512 devices in a mesh: tm: 8 (over y_hi, core), space: 64 (over y_lo, x, z).
Axes of the slice: x: 4, y: 8 (y_hi: 4, y_lo: 2; y = y_hi * 2 + y_lo), z: 8, core: 2. Of those that a mesh axis runs over, the one named last changes fastest.
Arguments:
- window_start: float32 [8, 64, 16, 32, 128], P('tm', 'space'), may hold values from -6 to 6
- courant_x: float32 [8, 64, 16, 32, 128], P('tm', 'space'), may hold values from -0.3 to 0.3
- courant_y: float32 [8, 64, 16, 32, 128], P('tm', 'space'), may hold values from -0.3 to 0.3
Outputs:
- window_end: float32 [8, 64, 16, 32, 128], P('tm', 'space')
The draws below stay inside these ranges and needn't reach their ends.
All inputs are finite; a program needn't handle non-finite values.
Results may differ from the reference program's by a relative error of at most 0.00002.
Values sent between devices are 32-bit elements; how exact they have to be, the bound alone decides.
A program may use at most 64 MiB of HBM per device.

```python
import jax
import jax.numpy as jnp
from jax import lax

CX = 32
CY = 128
NZ = 16
STEPS = 16
ITERS = 2
TILES_X = 8
TILES = 64
NWIN = 8


def shard_levels(stream_key, extent, pieces, least, top_value):
    def one(position, blocks):
        draws = jax.random.uniform(jax.random.fold_in(jax.random.fold_in(stream_key, 6), position), (blocks,), jnp.float32, least / len(pieces), top_value / len(pieces))
        return jnp.repeat(jnp.exp(draws), extent[position] // blocks).reshape((-1,) + (1,) * (len(extent) - position - 1))

    gain = one(*pieces[0])
    for cut in pieces[1:]:
        gain = gain * one(*cut)
    return gain


def noise(stream_key, dims, scale, bound, split=(), held_as=jnp.bfloat16):
    factor_of = shard_levels(stream_key, dims, split, -0.22, 0.18) if split else 1.0
    entries = jax.random.normal(stream_key, dims, jnp.float32) * scale * factor_of
    return jnp.minimum(jnp.maximum(entries, -bound), bound).astype(held_as)


def setup_inputs(seed: int = 0) -> dict:
    keys = jax.random.split(jax.random.key(seed), 4)
    window_start = noise(keys[0], (NWIN, TILES, NZ, CX, CY), 1.0, 6.0, ((0, 8), (1, 64)), jnp.float32)
    courant_x = jnp.clip(jax.random.uniform(keys[1], (NWIN, TILES, NZ, CX, CY), jnp.float32, -0.3, 0.3) * shard_levels(keys[1], (NWIN, TILES, NZ, CX, CY), ((0, 8), (1, 64)), -0.4, 0.0), -0.3, 0.3)
    courant_y = jnp.clip(jax.random.uniform(keys[2], (NWIN, TILES, NZ, CX, CY), jnp.float32, -0.3, 0.3) * shard_levels(keys[2], (NWIN, TILES, NZ, CX, CY), ((0, 8), (1, 64)), -0.4, 0.0), -0.3, 0.3)
    return {"window_start": window_start, "courant_x": courant_x, "courant_y": courant_y}


horiz_mix = 0.06
vert_mix = 0.08
robin_coef = 0.6


def robin_data(inner, second):
    return inner * (1.5 * robin_coef - 1.0) + second * (1.0 - 0.5 * robin_coef)


def advance(field, flow_x, flow_y, ghost_east, ghost_west, ghost_north, ghost_south):
    plus_x = jnp.concatenate([field[..., 1:, :], ghost_east[..., None, :]], axis=-2)
    minus_x = jnp.concatenate([ghost_west[..., None, :], field[..., :-1, :]], axis=-2)
    plus_y = jnp.concatenate([field[..., 1:], ghost_north[..., None]], axis=-1)
    minus_y = jnp.concatenate([ghost_south[..., None], field[..., :-1]], axis=-1)
    plus_z = jnp.concatenate([field[..., 1:, :, :], field[..., -1:, :, :]], axis=-3)
    minus_z = jnp.concatenate([field[..., :1, :, :], field[..., :-1, :, :]], axis=-3)
    advect = jnp.maximum(flow_x, 0.0) * (field - minus_x) + jnp.minimum(flow_x, 0.0) * (plus_x - field)
    advect = advect + jnp.maximum(flow_y, 0.0) * (field - minus_y) + jnp.minimum(flow_y, 0.0) * (plus_y - field)
    spread = horiz_mix * (plus_x + minus_x + plus_y + minus_y - 4.0 * field)
    spread = spread + vert_mix * (plus_z + minus_z - 2.0 * field)
    return field - advect + spread


def run_window(start, flow_x, flow_y, data_east, data_west, data_north, data_south, has_east, has_west, has_north, has_south):
    keep_edge = 1.0 - 0.5 * robin_coef
    divisor = 1.0 + 0.5 * robin_coef

    def one_step(field, inputs):
        into_east, into_west, into_north, into_south = inputs
        ghost_east = has_east * (keep_edge * field[..., -1, :] + into_east) / divisor
        ghost_west = has_west * (keep_edge * field[..., 0, :] + into_west) / divisor
        ghost_north = has_north * (keep_edge * field[..., :, -1] + into_north) / divisor
        ghost_south = has_south * (keep_edge * field[..., :, 0] + into_south) / divisor
        edges = (field[..., 0, :], field[..., 1, :], field[..., -1, :], field[..., -2, :],
                 field[..., :, 0], field[..., :, 1], field[..., :, -1], field[..., :, -2])
        return advance(field, flow_x, flow_y, ghost_east, ghost_west, ghost_north, ghost_south), edges

    return lax.scan(one_step, start, (data_east, data_west, data_north, data_south))


def reference(window_start, courant_x, courant_y):
    tiles_y = TILES // TILES_X
    shaped = (NWIN, TILES_X, tiles_y, NZ, CX, CY)
    start = window_start.reshape(shaped)
    flow_x = courant_x.reshape(shaped)
    flow_y = courant_y.reshape(shaped)
    row_index = jnp.arange(TILES_X)[:, None] + jnp.zeros((1, tiles_y), jnp.int32)
    col_index = jnp.arange(tiles_y)[None, :] + jnp.zeros((TILES_X, 1), jnp.int32)
    has_east = (row_index < TILES_X - 1).astype(jnp.float32).reshape(1, TILES_X, tiles_y, 1, 1)
    has_west = (row_index > 0).astype(jnp.float32).reshape(1, TILES_X, tiles_y, 1, 1)
    has_north = (col_index < tiles_y - 1).astype(jnp.float32).reshape(1, TILES_X, tiles_y, 1, 1)
    has_south = (col_index > 0).astype(jnp.float32).reshape(1, TILES_X, tiles_y, 1, 1)
    data_x = jnp.zeros((STEPS, NWIN, TILES_X, tiles_y, NZ, CY), jnp.float32)
    data_y = jnp.zeros((STEPS, NWIN, TILES_X, tiles_y, NZ, CX), jnp.float32)
    data_east, data_west, data_north, data_south = data_x, data_x, data_y, data_y
    state = start
    ended = start
    for sweep in range(ITERS + 1):
        ended, edges = run_window(state, flow_x, flow_y, data_east, data_west, data_north, data_south,
                                  has_east, has_west, has_north, has_south)
        if sweep < ITERS:
            west_inner, west_second, east_inner, east_second, south_inner, south_second, north_inner, north_second = edges
            offer_west = robin_data(west_inner, west_second)
            offer_east = robin_data(east_inner, east_second)
            offer_south = robin_data(south_inner, south_second)
            offer_north = robin_data(north_inner, north_second)
            data_east = jnp.concatenate([offer_west[:, :, 1:], jnp.zeros_like(offer_west[:, :, :1])], axis=2)
            data_west = jnp.concatenate([jnp.zeros_like(offer_east[:, :, :1]), offer_east[:, :, :-1]], axis=2)
            data_north = jnp.concatenate([offer_south[:, :, :, 1:], jnp.zeros_like(offer_south[:, :, :, :1])], axis=3)
            data_south = jnp.concatenate([jnp.zeros_like(offer_north[:, :, :, :1]), offer_north[:, :, :, :-1]], axis=3)
            state = jnp.concatenate([start[:1], ended[:-1]], axis=0)
    return ended.reshape(window_start.shape)
```

```python
import functools

import jax
import jax.numpy as jnp
from jax import lax
from jax.experimental import pallas as pl
from jax.experimental.pallas import tpu as pltpu
from jax.sharding import PartitionSpec as P

STEPS = 16
ITERS = 2
TILES_X = 8
LEVELS, ROWS_X, ROWS_Y = 16, 32, 128
PARTS = 4
BLOCKS = ROWS_X // PARTS
FIRST = 8
PADDED = ROWS_Y + 16
GROUPS = ROWS_Y // 8

HORIZ, VERT, ROBIN = 0.06, 0.08, 0.6
KEEP = (1.0 - 0.5 * ROBIN) / (1.0 + 0.5 * ROBIN)
INNER = (1.5 * ROBIN - 1.0) / (1.0 + 0.5 * ROBIN)
SECOND = (1.0 - 0.5 * ROBIN) / (1.0 + 0.5 * ROBIN)
RESCALE = VERT**STEPS

MESH = pl.DeviceIdType.MESH
f32 = jnp.float32


def lane_ids():
    return lax.broadcasted_iota(jnp.int32, (8, 128), 1)


def step(src, dst, t, coefs, ghosts, offers, has_south, has_north, scale):
    a_ref, b_ref, c_ref, d_ref, e_ref = coefs
    lane = lane_ids()
    block = lane % BLOCKS
    first_block, last_block = block == 0, block == BLOCKS - 1
    above = jnp.where(lane < 128 - BLOCKS, lane + BLOCKS, lane)
    below = jnp.where(lane >= BLOCKS, lane - BLOCKS, lane)

    south, north = src[:, FIRST, :], src[:, FIRST + ROWS_Y - 1, :]
    if offers is not None:
        east_out, west_out, south_out, north_out = offers
        south_out[pl.ds(t * PARTS, PARTS), :] = south * INNER + src[:, FIRST + 1, :] * SECOND
        north_out[pl.ds(t * PARTS, PARTS), :] = (
            north * INNER + src[:, FIRST + ROWS_Y - 2, :] * SECOND
        )
    south_ghost, north_ghost = south * (KEEP * has_south), north * (KEEP * has_north)
    if ghosts is not None:
        east_in, west_in, south_in, north_in = ghosts
        south_ghost = south_ghost + south_in[pl.ds(t * PARTS, PARTS), :]
        north_ghost = north_ghost + north_in[pl.ds(t * PARTS, PARTS), :]
    src[:, FIRST - 1, :] = south_ghost
    src[:, FIRST + ROWS_Y, :] = north_ghost

    for group in range(GROUPS):
        page, spot = group // 8, group % 8
        row = FIRST + 8 * group
        own = slice(8 * group, 8 * group + 8)
        f = [src[i, row : row + 8, :] for i in range(PARTS)]
        past_east = pltpu.roll(f[0], 127, 1)
        past_west = pltpu.roll(f[3], 1, 1)
        if ghosts is not None:
            if spot == 0:
                east_data = east_in[pl.ds(t * 16 + page * 8, 8), :]
                west_data = west_in[pl.ds(t * 16 + page * 8, 8), :]
            into_east = east_data if spot == 7 else pltpu.roll(east_data, 7 - spot, 1)
            into_west = west_data if spot == 0 else pltpu.roll(west_data, 128 - spot, 1)
        else:
            into_east = into_west = 0.0
        past_east = jnp.where(last_block, into_east, past_east)
        past_west = jnp.where(first_block, into_west, past_west)
        plus_x = f[1:] + [past_east]
        minus_x = [past_west] + f[:-1]
        for i in range(PARTS):
            plus_z = jnp.take_along_axis(f[i], above, axis=1, mode="promise_in_bounds")
            minus_z = jnp.take_along_axis(f[i], below, axis=1, mode="promise_in_bounds")
            new = (
                (a_ref[i, own, :] * plus_x[i] + b_ref[i, own, :] * minus_x[i])
                + (
                    c_ref[i, own, :] * src[i, row + 1 : row + 9, :]
                    + d_ref[i, own, :] * src[i, row - 1 : row + 7, :]
                )
                + (e_ref[i, own, :] * f[i] + (plus_z + minus_z))
            )
            if scale is not None:
                new = new * scale
            dst[i, row : row + 8, :] = new
        if offers is not None:
            east = f[2] + f[3] * (INNER / SECOND)
            west = f[1] + f[0] * (INNER / SECOND)
            if spot != 7:
                east = pltpu.roll(east, 128 - (7 - spot), 1)
            if spot != 0:
                west = pltpu.roll(west, spot, 1)
            east_pack = east if spot == 0 else jnp.where(block == spot, east, east_pack)
            west_pack = west if spot == 0 else jnp.where(block == spot, west, west_pack)
            if spot == 7:
                east_out[pl.ds(t * 16 + page * 8, 8), :] = east_pack * SECOND
                west_out[pl.ds(t * 16 + page * 8, 8), :] = west_pack * SECOND


def kernel(
    tiles_y,
    windows,
    start_hbm,
    flow_x_hbm,
    flow_y_hbm,
    out,
    raw,
    fields,
    other,
    a_ref,
    b_ref,
    c_ref,
    d_ref,
    e_ref,
    x_out,
    x_in,
    y_out,
    y_in,
    load_sem,
    send_sem,
    recv_sem,
):
    window = lax.axis_index("tm")
    place = lax.axis_index("space")
    row, col = place // tiles_y, place % tiles_y
    has_east, has_west = row < TILES_X - 1, row > 0
    has_north, has_south = col < tiles_y - 1, col > 0
    has_later, has_earlier = window < windows - 1, window > 0
    to_east, to_west = {"space": place + tiles_y}, {"space": place - tiles_y}
    to_north, to_south = {"space": place + 1}, {"space": place - 1}
    to_later, to_earlier = {"tm": window + 1}, {"tm": window - 1}

    loads = [
        pltpu.make_async_copy(ref, raw.at[k], load_sem.at[k])
        for k, ref in enumerate((flow_x_hbm, flow_y_hbm, start_hbm))
    ]
    for load in loads:
        load.start()
    barrier = pltpu.get_barrier_semaphore()
    links = (
        (to_east, has_east),
        (to_west, has_west),
        (to_north, has_north),
        (to_south, has_south),
        (to_later, has_later),
        (to_earlier, has_earlier),
    )
    count = 0
    for device, there in links:
        @pl.when(there)
        def _():
            pl.semaphore_signal(barrier, inc=1, device_id=device, device_id_type=MESH)

        count = count + there.astype(jnp.int32)

    zero_x = jnp.zeros((STEPS * 16, 128), f32)
    zero_y = jnp.zeros((STEPS * PARTS, 128), f32)
    for k in range(ITERS):
        for side, there in ((0, has_east), (1, has_west)):
            @pl.when(jnp.logical_not(there))
            def _():
                x_in[k, side] = zero_x

        for side, there in ((0, has_south), (1, has_north)):
            @pl.when(jnp.logical_not(there))
            def _():
                y_in[k, side] = zero_y

    lane = lax.broadcasted_iota(jnp.int32, (ROWS_Y, 128), 1) % BLOCKS
    east_keep = jnp.where(lane == BLOCKS - 1, has_east.astype(f32) * KEEP, 0.0)
    west_keep = jnp.where(lane == 0, has_west.astype(f32) * KEEP, 0.0)
    loads[0].wait()
    loads[1].wait()
    for i in range(PARTS):
        cx = jnp.transpose(raw[0, pl.ds(i, 128, stride=PARTS), :]) * (1.0 / VERT)
        cy = jnp.transpose(raw[1, pl.ds(i, 128, stride=PARTS), :]) * (1.0 / VERT)
        mix = HORIZ / VERT
        a = mix - jnp.minimum(cx, 0.0)
        b = mix + jnp.maximum(cx, 0.0)
        e = ((1.0 - 4.0 * HORIZ - 2.0 * VERT) / VERT - jnp.abs(cx)) - jnp.abs(cy)
        if i == 0:
            e = e + b * west_keep
        if i == PARTS - 1:
            e = e + a * east_keep
        a_ref[i] = a
        b_ref[i] = b
        c_ref[i] = mix - jnp.minimum(cy, 0.0)
        d_ref[i] = mix + jnp.maximum(cy, 0.0)
        e_ref[i] = e
    loads[2].wait()
    for i in range(PARTS):
        fields[0, i, FIRST : FIRST + ROWS_Y, :] = jnp.transpose(
            raw[2, pl.ds(i, 128, stride=PARTS), :]
        )

    @pl.when(jnp.logical_not(has_earlier))
    def _():
        for k in range(ITERS):
            fields[k + 1, :, FIRST : FIRST + ROWS_Y, :] = fields[0, :, FIRST : FIRST + ROWS_Y, :]

    coefs = (a_ref, b_ref, c_ref, d_ref, e_ref)
    south_there, north_there = has_south.astype(f32), has_north.astype(f32)
    sends = []
    for sweep in range(ITERS + 1):
        field = fields.at[sweep]
        ghosts = offers = None
        if sweep > 0:
            for copy, _, arrives in sends:
                pl.when(arrives)(copy.wait_recv)
            k = sweep - 1
            ghosts = (x_in.at[k, 0], x_in.at[k, 1], y_in.at[k, 0], y_in.at[k, 1])
        if sweep < ITERS:
            k = sweep
            offers = (x_out.at[k, 0], x_out.at[k, 1], y_out.at[k, 0], y_out.at[k, 1])

        def pair(p, last):
            t = 2 * p
            step(field, other, t, coefs, ghosts, offers, south_there, north_there, None)
            step(
                other,
                field,
                t + 1,
                coefs,
                ghosts,
                offers,
                south_there,
                north_there,
                RESCALE if last else None,
            )

        @pl.loop(0, STEPS // 2 - 1)
        def _(p):
            pair(p, False)

        pair(STEPS // 2 - 1, True)

        if sweep == 0:
            pl.semaphore_wait(barrier, count)
        if sweep < ITERS:
            k = sweep
            inside = slice(FIRST, FIRST + ROWS_Y)
            routes = (
                (field.at[:, inside, :], fields.at[sweep + 1, :, inside, :], to_later, has_later, has_earlier),
                (x_out.at[k, 0], x_in.at[k, 1], to_east, has_east, has_west),
                (x_out.at[k, 1], x_in.at[k, 0], to_west, has_west, has_east),
                (y_out.at[k, 0], y_in.at[k, 1], to_south, has_south, has_north),
                (y_out.at[k, 1], y_in.at[k, 0], to_north, has_north, has_south),
            )
            sends = []
            for n, (source, target, device, leaves, arrives) in enumerate(routes):
                copy = pltpu.make_async_remote_copy(
                    src_ref=source,
                    dst_ref=target,
                    send_sem=send_sem.at[k, n],
                    recv_sem=recv_sem.at[k, n],
                    device_id=device,
                    device_id_type=MESH,
                )
                pl.when(leaves)(copy.start)
                sends.append((copy, leaves, arrives))
            if sweep == 0:
                first_sends = sends
    out[...] = fields[ITERS, :, FIRST : FIRST + ROWS_Y, :]
    for copy, leaves, _ in first_sends + sends:
        pl.when(leaves)(copy.wait_send)


def restore(field, out):
    for i in range(PARTS):
        out[pl.ds(i, 128, stride=PARTS), :] = jnp.transpose(field[i])


def body(window_start, courant_x, courant_y):
    cells = (LEVELS * ROWS_X, ROWS_Y)
    x_data = (ITERS, 2, STEPS * 16, 128)
    y_data = (ITERS, 2, STEPS * PARTS, 128)
    whole = (PARTS, ROWS_Y, 128)
    vmem = pl.BlockSpec(memory_space=pltpu.VMEM)
    field = pl.pallas_call(
        functools.partial(kernel, lax.axis_size("space") // TILES_X, lax.axis_size("tm")),
        out_shape=jax.ShapeDtypeStruct(whole, f32),
        in_specs=[pl.BlockSpec(memory_space=pl.ANY)] * 3,
        out_specs=vmem,
        scratch_shapes=[
            pltpu.VMEM((3,) + cells, f32),
            pltpu.VMEM((ITERS + 1, PARTS, PADDED, 128), f32),
            pltpu.VMEM((PARTS, PADDED, 128), f32),
            pltpu.VMEM(whole, f32),
            pltpu.VMEM(whole, f32),
            pltpu.VMEM(whole, f32),
            pltpu.VMEM(whole, f32),
            pltpu.VMEM(whole, f32),
            pltpu.VMEM(x_data, f32),
            pltpu.VMEM(x_data, f32),
            pltpu.VMEM(y_data, f32),
            pltpu.VMEM(y_data, f32),
            pltpu.SemaphoreType.DMA((3,)),
            pltpu.SemaphoreType.DMA((ITERS, 5)),
            pltpu.SemaphoreType.DMA((ITERS, 5)),
        ],
        compiler_params=pltpu.CompilerParams(
            collective_id=0, has_side_effects=True, vmem_limit_bytes=24 << 20
        ),
    )(window_start.reshape(cells), courant_x.reshape(cells), courant_y.reshape(cells))
    ended = pl.pallas_call(
        restore,
        out_shape=jax.ShapeDtypeStruct(cells, f32),
        in_specs=[vmem],
        out_specs=vmem,
    )(field)
    return ended.reshape(window_start.shape)


def solution(mesh):
    spec = P("tm", "space", None, None, None)
    return jax.shard_map(
        body, mesh=mesh, in_specs=(spec, spec, spec), out_specs=spec, check_vma=False
    )
```

```python
import functools

import jax
import jax.numpy as jnp
from jax import lax
from jax.experimental import pallas as pl
from jax.experimental.pallas import tpu as pltpu
from jax.sharding import PartitionSpec as P

STEPS = 16
ITERS = 2
TILES_X = 8
LEVELS, ROWS_X, ROWS_Y = 16, 32, 128
SIDE = 4
SLABS = SIDE * SIDE
FIRST = 8
PADDED = ROWS_X + 16
GROUPS = ROWS_X // 8
HALF = STEPS // 2

HORIZ, VERT, ROBIN = 0.06, 0.08, 0.6
KEEP = (1.0 - 0.5 * ROBIN) / (1.0 + 0.5 * ROBIN)
INNER = (1.5 * ROBIN - 1.0) / (1.0 + 0.5 * ROBIN)
SECOND = (1.0 - 0.5 * ROBIN) / (1.0 + 0.5 * ROBIN)
RESCALE = VERT**STEPS

MESH = pl.DeviceIdType.MESH
f32 = jnp.float32


def lane_ids():
    return lax.broadcasted_iota(jnp.int32, (8, 128), 1)


def turn(x, by):
    return pltpu.roll(x, by % 128, 1) if by % 128 else x


def swapped(v):
    lane = lane_ids()
    low, high = lane % 2 == 0, lane % 4 < 2
    t0 = jnp.where(low, v[0], turn(v[1], 1))
    t1 = jnp.where(low, turn(v[0], -1), v[1])
    t2 = jnp.where(low, v[2], turn(v[3], 1))
    t3 = jnp.where(low, turn(v[2], -1), v[3])
    return (
        jnp.where(high, t0, turn(t2, 2)),
        jnp.where(high, t1, turn(t3, 2)),
        jnp.where(high, turn(t0, -2), t2),
        jnp.where(high, turn(t1, -2), t3),
    )


def side_rows(ref, row):
    return ref.at[pl.ds(row, SLABS, stride=PADDED), :]


def step(src, dst, t, coefs, ghosts, offers, scale):
    a_ref, b_ref, c_ref, d_ref, e_ref = coefs
    lane = lane_ids()
    north_side, south_side = lane >= 128 - SIDE, lane < SIDE
    top, bottom = lane % SIDE == SIDE - 1, lane % SIDE == 0
    south_data = lane % 8 < SIDE

    if offers is not None:
        east_out, west_out, y_out = offers
        west_out[pl.ds(t * SLABS, SLABS), :] = (
            side_rows(src, FIRST)[...] * INNER + side_rows(src, FIRST + 1)[...] * SECOND
        )
        east_out[pl.ds(t * SLABS, SLABS), :] = (
            side_rows(src, FIRST + ROWS_X - 1)[...] * INNER
            + side_rows(src, FIRST + ROWS_X - 2)[...] * SECOND
        )
    if ghosts is not None:
        east_in, west_in, south_in, north_in = ghosts
        side_rows(src, FIRST - 1)[...] = west_in[pl.ds(t * SLABS, SLABS), :]
        side_rows(src, FIRST + ROWS_X)[...] = east_in[pl.ds(t * SLABS, SLABS), :]
        both = jnp.where(
            south_data,
            turn(north_in[pl.ds(t * 8, 8), :], -SIDE),
            turn(south_in[pl.ds(t * 8, 8), :], SIDE),
        )

    packed = None
    for group in range(GROUPS):
        own = slice(8 * group, 8 * group + 8)
        f = []
        for iz in range(SIDE):
            base = [(SIDE * iz + iy) * PADDED + FIRST + 8 * group for iy in range(SIDE)]
            f.append([src[b : b + 8, :] for b in base])
        for iz in range(SIDE):
            spot = SIDE * group + iz
            ghost = 0.0 if ghosts is None else turn(both, -8 * spot - SIDE)
            past_north = jnp.where(north_side, ghost, turn(f[iz][0], -SIDE))
            past_south = jnp.where(south_side, ghost, turn(f[iz][3], SIDE))
            plus_y = f[iz][1:] + [past_north]
            minus_y = [past_south] + f[iz][:-1]
            for iy in range(SIDE):
                slab = SIDE * iz + iy
                base = slab * PADDED + FIRST + 8 * group
                if iz == SIDE - 1:
                    plus_z = jnp.where(top, f[iz][iy], turn(f[0][iy], -1))
                else:
                    plus_z = f[iz + 1][iy]
                if iz == 0:
                    minus_z = jnp.where(bottom, f[iz][iy], turn(f[SIDE - 1][iy], 1))
                else:
                    minus_z = f[iz - 1][iy]
                new = (
                    (
                        a_ref[slab, own, :] * src[base + 1 : base + 9, :]
                        + b_ref[slab, own, :] * src[base - 1 : base + 7, :]
                    )
                    + (c_ref[slab, own, :] * plus_y[iy] + d_ref[slab, own, :] * minus_y[iy])
                    + (e_ref[slab, own, :] * f[iz][iy] + (plus_z + minus_z))
                )
                if scale is not None:
                    new = new * scale
                dst[base : base + 8, :] = new
            if offers is not None:
                first = jnp.where(north_side, f[iz][3], f[iz][0])
                second = jnp.where(north_side, f[iz][2], f[iz][1])
                offer = turn(second + first * (INNER / SECOND), 8 * spot + SIDE)
                packed = offer if packed is None else jnp.where(lane // 8 == spot, offer, packed)
    if offers is not None:
        y_out[pl.ds(t * 8, 8), :] = packed * SECOND


def kernel(
    tiles_y,
    windows,
    start_hbm,
    flow_x_hbm,
    flow_y_hbm,
    out,
    raw,
    fields,
    other,
    a_ref,
    b_ref,
    c_ref,
    d_ref,
    e_ref,
    x_out,
    x_in,
    y_out,
    y_in,
    load_sem,
    send_sem,
    recv_sem,
):
    window = lax.axis_index("tm")
    place = lax.axis_index("space")
    row, col = place // tiles_y, place % tiles_y
    has_east, has_west = row < TILES_X - 1, row > 0
    has_north, has_south = col < tiles_y - 1, col > 0
    has_later, has_earlier = window < windows - 1, window > 0
    to_east, to_west = {"space": place + tiles_y}, {"space": place - tiles_y}
    to_north, to_south = {"space": place + 1}, {"space": place - 1}
    to_later, to_earlier = {"tm": window + 1}, {"tm": window - 1}

    loads = [
        pltpu.make_async_copy(ref, raw.at[k], load_sem.at[k])
        for k, ref in enumerate((flow_x_hbm, flow_y_hbm, start_hbm))
    ]
    for load in loads:
        load.start()
    barrier = pltpu.get_barrier_semaphore()
    links = (
        (to_east, has_east),
        (to_west, has_west),
        (to_north, has_north),
        (to_south, has_south),
        (to_later, has_later),
        (to_earlier, has_earlier),
    )
    count = 0
    for device, there in links:
        @pl.when(there)
        def _():
            pl.semaphore_signal(barrier, inc=1, device_id=device, device_id_type=MESH)

        count = count + there.astype(jnp.int32)

    zero_row = jnp.zeros((SLABS, 128), f32)
    for ref in (fields.at[0], other):
        side_rows(ref, FIRST - 1)[...] = zero_row
        side_rows(ref, FIRST + ROWS_X)[...] = zero_row
    zero_x = jnp.zeros((STEPS * SLABS, 128), f32)
    zero_y = jnp.zeros((STEPS * 8, 128), f32)
    for k in range(ITERS):
        for side, there in ((0, has_east), (1, has_west)):
            @pl.when(jnp.logical_not(there))
            def _():
                x_in[k, side] = zero_x

        for side, there in ((0, has_south), (1, has_north)):
            @pl.when(jnp.logical_not(there))
            def _():
                y_in[k, side] = zero_y

    lane = lane_ids()
    sub = lax.broadcasted_iota(jnp.int32, (8, 128), 0)
    east_keep = jnp.where(sub == 7, has_east.astype(f32) * KEEP, 0.0)
    west_keep = jnp.where(sub == 0, has_west.astype(f32) * KEEP, 0.0)
    north_keep = jnp.where(lane >= 128 - SIDE, has_north.astype(f32) * KEEP, 0.0)
    south_keep = jnp.where(lane < SIDE, has_south.astype(f32) * KEEP, 0.0)

    def gathered(which, group, iz):
        rows = [(SIDE * zb + iz) * ROWS_X + 8 * group for zb in range(SIDE)]
        return swapped([raw[which, r : r + 8, :] for r in rows])

    loads[0].wait()
    loads[1].wait()
    mix = HORIZ / VERT
    for group in range(GROUPS):
        own = slice(8 * group, 8 * group + 8)
        for iz in range(SIDE):
            flow_x, flow_y = gathered(0, group, iz), gathered(1, group, iz)
            for iy in range(SIDE):
                slab = SIDE * iz + iy
                cx, cy = flow_x[iy] * (1.0 / VERT), flow_y[iy] * (1.0 / VERT)
                a = mix - jnp.minimum(cx, 0.0)
                b = mix + jnp.maximum(cx, 0.0)
                c = mix - jnp.minimum(cy, 0.0)
                d = mix + jnp.maximum(cy, 0.0)
                e = ((1.0 - 4.0 * HORIZ - 2.0 * VERT) / VERT - jnp.abs(cx)) - jnp.abs(cy)
                if group == GROUPS - 1:
                    e = e + a * east_keep
                if group == 0:
                    e = e + b * west_keep
                if iy == SIDE - 1:
                    e = e + c * north_keep
                if iy == 0:
                    e = e + d * south_keep
                a_ref[slab, own, :] = a
                b_ref[slab, own, :] = b
                c_ref[slab, own, :] = c
                d_ref[slab, own, :] = d
                e_ref[slab, own, :] = e
    loads[2].wait()
    for group in range(GROUPS):
        for iz in range(SIDE):
            start = gathered(2, group, iz)
            for iy in range(SIDE):
                base = (SIDE * iz + iy) * PADDED + FIRST + 8 * group
                fields[0, base : base + 8, :] = start[iy]

    @pl.when(jnp.logical_not(has_earlier))
    def _():
        for k in range(ITERS):
            for slab in range(SLABS):
                inside = slice(slab * PADDED + FIRST, slab * PADDED + FIRST + ROWS_X)
                fields[k + 1, inside, :] = fields[0, inside, :]

    coefs = (a_ref, b_ref, c_ref, d_ref, e_ref)
    started = []

    def send(k, n, source, target, device, leaves, arrives):
        copy = pltpu.make_async_remote_copy(
            src_ref=source,
            dst_ref=target,
            send_sem=send_sem.at[k, n],
            recv_sem=recv_sem.at[k, n],
            device_id=device,
            device_id_type=MESH,
        )
        pl.when(leaves)(copy.start)
        started.append((copy, leaves))
        return copy, arrives

    def send_sides(k, part):
        x_part = pl.ds(part * HALF * SLABS, HALF * SLABS)
        y_part = pl.ds(part * HALF * 8, HALF * 8)
        n = 1 + 4 * part
        return [
            send(k, n, x_out.at[k, 0, x_part], x_in.at[k, 1, x_part], to_east, has_east, has_west),
            send(k, n + 1, x_out.at[k, 1, x_part], x_in.at[k, 0, x_part], to_west, has_west, has_east),
            send(k, n + 2, y_out.at[k, y_part], y_in.at[k, 1, y_part], to_south, has_south, has_north),
            send(k, n + 3, y_out.at[k, y_part], y_in.at[k, 0, y_part], to_north, has_north, has_south),
        ]

    def receive(copies):
        for copy, arrives in copies:
            pl.when(arrives)(copy.wait_recv)

    early = late = None
    for sweep in range(ITERS + 1):
        field = fields.at[sweep]
        ghosts = offers = None
        if sweep > 0:
            receive(early)
            k = sweep - 1
            ghosts = (x_in.at[k, 0], x_in.at[k, 1], y_in.at[k, 0], y_in.at[k, 1])
        if sweep < ITERS:
            offers = (x_out.at[sweep, 0], x_out.at[sweep, 1], y_out.at[sweep])

        def pair(p, scale=None):
            step(field, other, 2 * p, coefs, ghosts, offers, None)
            step(other, field, 2 * p + 1, coefs, ghosts, offers, scale)

        pl.loop(0, HALF // 2)(pair)
        if sweep > 0:
            receive(late)
        if sweep == 0:
            pl.semaphore_wait(barrier, count)
        if sweep < ITERS:
            early = send_sides(sweep, 0)
        pl.loop(HALF // 2, HALF - 1)(pair)
        pair(HALF - 1, RESCALE)
        if sweep < ITERS:
            inside = slice(FIRST, FIRST + ROWS_X)
            ended = field.reshape(SLABS, PADDED, 128).at[:, inside, :]
            landing = fields.at[sweep + 1].reshape(SLABS, PADDED, 128).at[:, inside, :]
            early.append(send(sweep, 0, ended, landing, to_later, has_later, has_earlier))
            late = send_sides(sweep, 1)

    for group in range(GROUPS):
        for iz in range(SIDE):
            base = [(SIDE * iz + iy) * PADDED + FIRST + 8 * group for iy in range(SIDE)]
            ended = swapped([fields[ITERS, b : b + 8, :] for b in base])
            for zb in range(SIDE):
                r = (SIDE * zb + iz) * ROWS_X + 8 * group
                out[r : r + 8, :] = ended[zb]
    for copy, leaves in started:
        pl.when(leaves)(copy.wait_send)


def body(window_start, courant_x, courant_y):
    cells = (LEVELS * ROWS_X, ROWS_Y)
    coef = pltpu.VMEM((SLABS, ROWS_X, 128), f32)
    ended = pl.pallas_call(
        functools.partial(kernel, lax.axis_size("space") // TILES_X, lax.axis_size("tm")),
        out_shape=jax.ShapeDtypeStruct(cells, f32),
        in_specs=[pl.BlockSpec(memory_space=pl.ANY)] * 3,
        out_specs=pl.BlockSpec(memory_space=pltpu.VMEM),
        scratch_shapes=[
            pltpu.VMEM((3,) + cells, f32),
            pltpu.VMEM((ITERS + 1, SLABS * PADDED, 128), f32),
            pltpu.VMEM((SLABS * PADDED, 128), f32),
            coef,
            coef,
            coef,
            coef,
            coef,
            pltpu.VMEM((ITERS, 2, STEPS * SLABS, 128), f32),
            pltpu.VMEM((ITERS, 2, STEPS * SLABS, 128), f32),
            pltpu.VMEM((ITERS, STEPS * 8, 128), f32),
            pltpu.VMEM((ITERS, 2, STEPS * 8, 128), f32),
            pltpu.SemaphoreType.DMA((3,)),
            pltpu.SemaphoreType.DMA((ITERS, 9)),
            pltpu.SemaphoreType.DMA((ITERS, 9)),
        ],
        compiler_params=pltpu.CompilerParams(
            collective_id=0, has_side_effects=True, vmem_limit_bytes=56 << 20
        ),
    )(window_start.reshape(cells), courant_x.reshape(cells), courant_y.reshape(cells))
    return ended.reshape(window_start.shape)


def solution(mesh):
    spec = P("tm", "space", None, None, None)
    return jax.shard_map(
        body, mesh=mesh, in_specs=(spec, spec, spec), out_specs=spec, check_vma=False
    )
```

```python
import functools

import jax
import jax.numpy as jnp
from jax import lax
from jax.experimental import pallas as pl
from jax.experimental.pallas import tpu as pltpu
from jax.sharding import PartitionSpec as P

STEPS = 16
ITERS = 2
TILES_X = 8
LEVELS, ROWS_X, ROWS_Y = 16, 32, 128
SIDE = 4
SLABS = SIDE * SIDE
FIRST = 8
PADDED = ROWS_X + 16
GROUPS = ROWS_X // 8
SPAN = 4
SPANS = STEPS // SPAN

HORIZ, VERT, ROBIN = 0.06, 0.08, 0.6
KEEP = (1.0 - 0.5 * ROBIN) / (1.0 + 0.5 * ROBIN)
INNER = (1.5 * ROBIN - 1.0) / (1.0 + 0.5 * ROBIN)
SECOND = (1.0 - 0.5 * ROBIN) / (1.0 + 0.5 * ROBIN)
RESCALE = VERT**STEPS

MESH = pl.DeviceIdType.MESH
f32 = jnp.float32


def lane_ids():
    return lax.broadcasted_iota(jnp.int32, (8, 128), 1)


def turn(x, by):
    return pltpu.roll(x, by % 128, 1) if by % 128 else x


def swapped(v):
    lane = lane_ids()
    low, high = lane % 2 == 0, lane % 4 < 2
    t0 = jnp.where(low, v[0], turn(v[1], 1))
    t1 = jnp.where(low, turn(v[0], -1), v[1])
    t2 = jnp.where(low, v[2], turn(v[3], 1))
    t3 = jnp.where(low, turn(v[2], -1), v[3])
    return (
        jnp.where(high, t0, turn(t2, 2)),
        jnp.where(high, t1, turn(t3, 2)),
        jnp.where(high, turn(t0, -2), t2),
        jnp.where(high, turn(t1, -2), t3),
    )


def side_rows(ref, row):
    return ref.at[pl.ds(row, SLABS, stride=PADDED), :]


def step(src, dst, t, coefs, ghosts, offers, scale):
    a_ref, b_ref, c_ref, d_ref, e_ref = coefs
    lane = lane_ids()
    north_side, south_side = lane >= 128 - SIDE, lane < SIDE
    top, bottom = lane % SIDE == SIDE - 1, lane % SIDE == 0
    south_data = lane % 8 < SIDE

    if offers is not None:
        east_out, west_out, y_out = offers
        west_out[pl.ds(t * SLABS, SLABS), :] = (
            side_rows(src, FIRST)[...] * INNER + side_rows(src, FIRST + 1)[...] * SECOND
        )
        east_out[pl.ds(t * SLABS, SLABS), :] = (
            side_rows(src, FIRST + ROWS_X - 1)[...] * INNER
            + side_rows(src, FIRST + ROWS_X - 2)[...] * SECOND
        )
    if ghosts is not None:
        east_in, west_in, south_in, north_in = ghosts
        side_rows(src, FIRST - 1)[...] = west_in[pl.ds(t * SLABS, SLABS), :]
        side_rows(src, FIRST + ROWS_X)[...] = east_in[pl.ds(t * SLABS, SLABS), :]
        both = jnp.where(
            south_data,
            turn(north_in[pl.ds(t * 8, 8), :], -SIDE),
            turn(south_in[pl.ds(t * 8, 8), :], SIDE),
        )

    packed = None
    for group in range(GROUPS):
        own = slice(8 * group, 8 * group + 8)
        f = []
        for iz in range(SIDE):
            base = [(SIDE * iz + iy) * PADDED + FIRST + 8 * group for iy in range(SIDE)]
            f.append([src[b : b + 8, :] for b in base])
        for iz in range(SIDE):
            spot = SIDE * group + iz
            ghost = 0.0 if ghosts is None else turn(both, -8 * spot - SIDE)
            past_north = jnp.where(north_side, ghost, turn(f[iz][0], -SIDE))
            past_south = jnp.where(south_side, ghost, turn(f[iz][3], SIDE))
            plus_y = f[iz][1:] + [past_north]
            minus_y = [past_south] + f[iz][:-1]
            for iy in range(SIDE):
                slab = SIDE * iz + iy
                base = slab * PADDED + FIRST + 8 * group
                if iz == SIDE - 1:
                    plus_z = jnp.where(top, f[iz][iy], turn(f[0][iy], -1))
                else:
                    plus_z = f[iz + 1][iy]
                if iz == 0:
                    minus_z = jnp.where(bottom, f[iz][iy], turn(f[SIDE - 1][iy], 1))
                else:
                    minus_z = f[iz - 1][iy]
                new = (
                    (
                        a_ref[slab, own, :] * src[base + 1 : base + 9, :]
                        + b_ref[slab, own, :] * src[base - 1 : base + 7, :]
                    )
                    + (c_ref[slab, own, :] * plus_y[iy] + d_ref[slab, own, :] * minus_y[iy])
                    + (e_ref[slab, own, :] * f[iz][iy] + (plus_z + minus_z))
                )
                if scale is not None:
                    new = new * scale
                dst[base : base + 8, :] = new
            if offers is not None:
                first = jnp.where(north_side, f[iz][3], f[iz][0])
                second = jnp.where(north_side, f[iz][2], f[iz][1])
                offer = turn(second + first * (INNER / SECOND), 8 * spot + SIDE)
                packed = offer if packed is None else jnp.where(lane // 8 == spot, offer, packed)
    if offers is not None:
        y_out[pl.ds(t * 8, 8), :] = packed * SECOND


def kernel(
    tiles_y,
    windows,
    start_hbm,
    flow_x_hbm,
    flow_y_hbm,
    out,
    raw,
    fields,
    other,
    a_ref,
    b_ref,
    c_ref,
    d_ref,
    e_ref,
    x_out,
    x_in,
    y_out,
    y_in,
    load_sem,
    send_sem,
    recv_sem,
    field_sem,
):
    window = lax.axis_index("tm")
    place = lax.axis_index("space")
    row, col = place // tiles_y, place % tiles_y
    has_east, has_west = row < TILES_X - 1, row > 0
    has_north, has_south = col < tiles_y - 1, col > 0
    has_later, has_earlier = window < windows - 1, window > 0
    to_east, to_west = {"space": place + tiles_y}, {"space": place - tiles_y}
    to_north, to_south = {"space": place + 1}, {"space": place - 1}
    to_later, to_earlier = {"tm": window + 1}, {"tm": window - 1}

    loads = [
        pltpu.make_async_copy(ref, raw.at[k], load_sem.at[k])
        for k, ref in enumerate((flow_x_hbm, flow_y_hbm, start_hbm))
    ]
    for load in loads:
        load.start()
    barrier = pltpu.get_barrier_semaphore()
    links = (
        (to_east, has_east),
        (to_west, has_west),
        (to_north, has_north),
        (to_south, has_south),
        (to_later, has_later),
        (to_earlier, has_earlier),
    )
    count = 0
    for device, there in links:
        @pl.when(there)
        def _():
            pl.semaphore_signal(barrier, inc=1, device_id=device, device_id_type=MESH)

        count = count + there.astype(jnp.int32)

    zero_row = jnp.zeros((SLABS, 128), f32)
    for ref in (fields.at[0], other):
        side_rows(ref, FIRST - 1)[...] = zero_row
        side_rows(ref, FIRST + ROWS_X)[...] = zero_row
    zero_x = jnp.zeros((STEPS * SLABS, 128), f32)
    zero_y = jnp.zeros((STEPS * 8, 128), f32)
    for k in range(ITERS):
        for side, there in ((0, has_east), (1, has_west)):
            @pl.when(jnp.logical_not(there))
            def _():
                x_in[k, side] = zero_x

        for side, there in ((0, has_south), (1, has_north)):
            @pl.when(jnp.logical_not(there))
            def _():
                y_in[k, side] = zero_y

    lane = lane_ids()
    sub = lax.broadcasted_iota(jnp.int32, (8, 128), 0)
    east_keep = jnp.where(sub == 7, has_east.astype(f32) * KEEP, 0.0)
    west_keep = jnp.where(sub == 0, has_west.astype(f32) * KEEP, 0.0)
    north_keep = jnp.where(lane >= 128 - SIDE, has_north.astype(f32) * KEEP, 0.0)
    south_keep = jnp.where(lane < SIDE, has_south.astype(f32) * KEEP, 0.0)

    def gathered(which, group, iz):
        rows = [(SIDE * zb + iz) * ROWS_X + 8 * group for zb in range(SIDE)]
        return swapped([raw[which, r : r + 8, :] for r in rows])

    loads[0].wait()
    loads[1].wait()
    mix = HORIZ / VERT
    for group in range(GROUPS):
        own = slice(8 * group, 8 * group + 8)
        for iz in range(SIDE):
            flow_x, flow_y = gathered(0, group, iz), gathered(1, group, iz)
            for iy in range(SIDE):
                slab = SIDE * iz + iy
                cx, cy = flow_x[iy] * (1.0 / VERT), flow_y[iy] * (1.0 / VERT)
                a = mix - jnp.minimum(cx, 0.0)
                b = mix + jnp.maximum(cx, 0.0)
                c = mix - jnp.minimum(cy, 0.0)
                d = mix + jnp.maximum(cy, 0.0)
                e = ((1.0 - 4.0 * HORIZ - 2.0 * VERT) / VERT - jnp.abs(cx)) - jnp.abs(cy)
                if group == GROUPS - 1:
                    e = e + a * east_keep
                if group == 0:
                    e = e + b * west_keep
                if iy == SIDE - 1:
                    e = e + c * north_keep
                if iy == 0:
                    e = e + d * south_keep
                a_ref[slab, own, :] = a
                b_ref[slab, own, :] = b
                c_ref[slab, own, :] = c
                d_ref[slab, own, :] = d
                e_ref[slab, own, :] = e
    loads[2].wait()
    for group in range(GROUPS):
        for iz in range(SIDE):
            start = gathered(2, group, iz)
            for iy in range(SIDE):
                base = (SIDE * iz + iy) * PADDED + FIRST + 8 * group
                fields[0, base : base + 8, :] = start[iy]

    @pl.when(jnp.logical_not(has_earlier))
    def _():
        for k in range(ITERS):
            for slab in range(SLABS):
                inside = slice(slab * PADDED + FIRST, slab * PADDED + FIRST + ROWS_X)
                fields[k + 1, inside, :] = fields[0, inside, :]

    coefs = (a_ref, b_ref, c_ref, d_ref, e_ref)

    def routed(source, target, sent, received, device, leaves, arrives):
        copy = pltpu.make_async_remote_copy(
            src_ref=source,
            dst_ref=target,
            send_sem=sent,
            recv_sem=received,
            device_id=device,
            device_id_type=MESH,
        )
        return copy, leaves, arrives

    def sides(k, part):
        x_part = pl.ds(part * SPAN * SLABS, SPAN * SLABS)
        y_part = pl.ds(part * SPAN * 8, SPAN * 8)
        routes = (
            (x_out.at[k, 0, x_part], x_in.at[k, 1, x_part], to_east, has_east, has_west),
            (x_out.at[k, 1, x_part], x_in.at[k, 0, x_part], to_west, has_west, has_east),
            (y_out.at[k, y_part], y_in.at[k, 1, y_part], to_south, has_south, has_north),
            (y_out.at[k, y_part], y_in.at[k, 0, y_part], to_north, has_north, has_south),
        )
        return [
            routed(source, target, send_sem.at[k, part, n], recv_sem.at[k, part, n], *rest)
            for n, (source, target, *rest) in enumerate(routes)
        ]

    def ended(k):
        inside = slice(FIRST, FIRST + ROWS_X)
        source, target = (
            fields.at[n].reshape(SLABS, PADDED, 128).at[:, inside, :] for n in (k, k + 1)
        )
        return [
            routed(
                source, target, field_sem.at[0, k], field_sem.at[1, k], to_later, has_later, has_earlier
            )
        ]

    def start(copies):
        for copy, leaves, _ in copies:
            pl.when(leaves)(copy.start)

    def arrive(copies):
        for copy, _, arrives in copies:
            pl.when(arrives)(copy.wait_recv)

    def leave(copies):
        for copy, leaves, _ in copies:
            pl.when(leaves)(copy.wait_send)

    for sweep in range(ITERS + 1):
        field = fields.at[sweep]
        ghosts = offers = None
        if sweep > 0:
            k = sweep - 1
            ghosts = (x_in.at[k, 0], x_in.at[k, 1], y_in.at[k, 0], y_in.at[k, 1])
            arrive(ended(k))
        if sweep < ITERS:
            offers = (x_out.at[sweep, 0], x_out.at[sweep, 1], y_out.at[sweep])

        def run(part, scale=None):
            if sweep > 0:
                arrive(sides(sweep - 1, part))
            for n in range(0, SPAN, 2):
                t = part * SPAN + n
                last = scale if n == SPAN - 2 else None
                step(field, other, t, coefs, ghosts, offers, None)
                step(other, field, t + 1, coefs, ghosts, offers, last)

        @pl.loop(0, SPANS - 1)
        def _(part):
            run(part)
            if sweep == 0:
                @pl.when(part == 0)
                def _():
                    pl.semaphore_wait(barrier, count)

            if sweep < ITERS:
                start(sides(sweep, part))

        run(SPANS - 1, RESCALE)
        if sweep < ITERS:
            start(ended(sweep))
            start(sides(sweep, SPANS - 1))

    for group in range(GROUPS):
        for iz in range(SIDE):
            base = [(SIDE * iz + iy) * PADDED + FIRST + 8 * group for iy in range(SIDE)]
            final = swapped([fields[ITERS, b : b + 8, :] for b in base])
            for zb in range(SIDE):
                r = (SIDE * zb + iz) * ROWS_X + 8 * group
                out[r : r + 8, :] = final[zb]
    for k in range(ITERS):
        leave(ended(k))

        @pl.loop(0, SPANS)
        def _(part):
            leave(sides(k, part))


def body(window_start, courant_x, courant_y):
    cells = (LEVELS * ROWS_X, ROWS_Y)
    coef = pltpu.VMEM((SLABS, ROWS_X, 128), f32)
    ended = pl.pallas_call(
        functools.partial(kernel, lax.axis_size("space") // TILES_X, lax.axis_size("tm")),
        out_shape=jax.ShapeDtypeStruct(cells, f32),
        in_specs=[pl.BlockSpec(memory_space=pltpu.HBM)] * 3,
        out_specs=pl.BlockSpec(memory_space=pltpu.VMEM),
        scratch_shapes=[
            pltpu.VMEM((3,) + cells, f32),
            pltpu.VMEM((ITERS + 1, SLABS * PADDED, 128), f32),
            pltpu.VMEM((SLABS * PADDED, 128), f32),
            coef,
            coef,
            coef,
            coef,
            coef,
            pltpu.VMEM((ITERS, 2, STEPS * SLABS, 128), f32),
            pltpu.VMEM((ITERS, 2, STEPS * SLABS, 128), f32),
            pltpu.VMEM((ITERS, STEPS * 8, 128), f32),
            pltpu.VMEM((ITERS, 2, STEPS * 8, 128), f32),
            pltpu.SemaphoreType.DMA((3,)),
            pltpu.SemaphoreType.DMA((ITERS, SPANS, 4)),
            pltpu.SemaphoreType.DMA((ITERS, SPANS, 4)),
            pltpu.SemaphoreType.DMA((2, ITERS)),
        ],
        compiler_params=pltpu.CompilerParams(
            collective_id=0, has_side_effects=True, vmem_limit_bytes=56 << 20
        ),
    )(window_start.reshape(cells), courant_x.reshape(cells), courant_y.reshape(cells))
    return ended.reshape(window_start.shape)


def solution(mesh):
    spec = P("tm", "space", None, None, None)
    return jax.shard_map(
        body, mesh=mesh, in_specs=(spec, spec, spec), out_specs=spec, check_vma=False
    )
```

```python
import functools

import jax
import jax.numpy as jnp
from jax import lax
from jax.experimental import pallas as pl
from jax.experimental.pallas import tpu as pltpu
from jax.sharding import PartitionSpec as P

STEPS = 16
ITERS = 2
TILES_X = 8
LEVELS, ROWS_X, ROWS_Y = 16, 32, 128
SIDE = 4
SLABS = SIDE * SIDE
FIRST = 8
PADDED = ROWS_X + 16
GROUPS = ROWS_X // 8
SPAN = 4
SPANS = STEPS // SPAN

HORIZ, VERT, ROBIN = 0.06, 0.08, 0.6
KEEP = (1.0 - 0.5 * ROBIN) / (1.0 + 0.5 * ROBIN)
INNER = (1.5 * ROBIN - 1.0) / (1.0 + 0.5 * ROBIN)
SECOND = (1.0 - 0.5 * ROBIN) / (1.0 + 0.5 * ROBIN)
RESCALE = VERT**STEPS

MESH = pl.DeviceIdType.MESH
f32 = jnp.float32


def lane_ids():
    return lax.broadcasted_iota(jnp.int32, (8, 128), 1)


def turn(x, by):
    return pltpu.roll(x, by % 128, 1) if by % 128 else x


def swapped(v):
    lane = lane_ids()
    low, high = lane % 2 == 0, lane % 4 < 2
    t0 = jnp.where(low, v[0], turn(v[1], 1))
    t1 = jnp.where(low, turn(v[0], -1), v[1])
    t2 = jnp.where(low, v[2], turn(v[3], 1))
    t3 = jnp.where(low, turn(v[2], -1), v[3])
    return (
        jnp.where(high, t0, turn(t2, 2)),
        jnp.where(high, t1, turn(t3, 2)),
        jnp.where(high, turn(t0, -2), t2),
        jnp.where(high, turn(t1, -2), t3),
    )


def side_rows(ref, row):
    return ref.at[pl.ds(row, SLABS, stride=PADDED), :]


def step(src, dst, t, coefs, ghosts, offers, scale):
    a_ref, b_ref, c_ref, d_ref, e_ref = coefs
    lane = lane_ids()
    north_side, south_side = lane >= 128 - SIDE, lane < SIDE
    top, bottom = lane % SIDE == SIDE - 1, lane % SIDE == 0
    south_data = lane % 8 < SIDE

    if offers is not None:
        east_out, west_out, y_out = offers
        west_out[pl.ds(t * SLABS, SLABS), :] = (
            side_rows(src, FIRST)[...] * INNER + side_rows(src, FIRST + 1)[...] * SECOND
        )
        east_out[pl.ds(t * SLABS, SLABS), :] = (
            side_rows(src, FIRST + ROWS_X - 1)[...] * INNER
            + side_rows(src, FIRST + ROWS_X - 2)[...] * SECOND
        )
    if ghosts is not None:
        east_in, west_in, south_in, north_in = ghosts
        side_rows(src, FIRST - 1)[...] = west_in[pl.ds(t * SLABS, SLABS), :]
        side_rows(src, FIRST + ROWS_X)[...] = east_in[pl.ds(t * SLABS, SLABS), :]
        both = jnp.where(
            south_data,
            turn(north_in[pl.ds(t * 8, 8), :], -SIDE),
            turn(south_in[pl.ds(t * 8, 8), :], SIDE),
        )

    packed = None
    for group in range(GROUPS):
        own = slice(8 * group, 8 * group + 8)
        f = []
        for iz in range(SIDE):
            base = [(SIDE * iz + iy) * PADDED + FIRST + 8 * group for iy in range(SIDE)]
            f.append([src[b : b + 8, :] for b in base])
        for iz in range(SIDE):
            spot = SIDE * group + iz
            ghost = 0.0 if ghosts is None else turn(both, -8 * spot - SIDE)
            past_north = jnp.where(north_side, ghost, turn(f[iz][0], -SIDE))
            past_south = jnp.where(south_side, ghost, turn(f[iz][3], SIDE))
            plus_y = f[iz][1:] + [past_north]
            minus_y = [past_south] + f[iz][:-1]
            for iy in range(SIDE):
                slab = SIDE * iz + iy
                base = slab * PADDED + FIRST + 8 * group
                if iz == SIDE - 1:
                    plus_z = jnp.where(top, f[iz][iy], turn(f[0][iy], -1))
                else:
                    plus_z = f[iz + 1][iy]
                if iz == 0:
                    minus_z = jnp.where(bottom, f[iz][iy], turn(f[SIDE - 1][iy], 1))
                else:
                    minus_z = f[iz - 1][iy]
                new = (
                    (
                        a_ref[slab, own, :] * src[base + 1 : base + 9, :]
                        + b_ref[slab, own, :] * src[base - 1 : base + 7, :]
                    )
                    + (c_ref[slab, own, :] * plus_y[iy] + d_ref[slab, own, :] * minus_y[iy])
                    + (e_ref[slab, own, :] * f[iz][iy] + (plus_z + minus_z))
                )
                if scale is not None:
                    new = new * scale
                dst[base : base + 8, :] = new
            if offers is not None:
                first = jnp.where(north_side, f[iz][3], f[iz][0])
                second = jnp.where(north_side, f[iz][2], f[iz][1])
                offer = turn(second + first * (INNER / SECOND), 8 * spot + SIDE)
                packed = offer if packed is None else jnp.where(lane // 8 == spot, offer, packed)
    if offers is not None:
        y_out[pl.ds(t * 8, 8), :] = packed * SECOND


def kernel(
    tiles_y,
    windows,
    start_hbm,
    flow_x_hbm,
    flow_y_hbm,
    out,
    raw,
    fields,
    other,
    a_ref,
    b_ref,
    c_ref,
    d_ref,
    e_ref,
    x_out,
    x_in,
    y_out,
    y_in,
    load_sem,
    send_sem,
    recv_sem,
    field_sem,
):
    window = lax.axis_index("tm")
    place = lax.axis_index("space")
    row, col = place // tiles_y, place % tiles_y
    has_east, has_west = row < TILES_X - 1, row > 0
    has_north, has_south = col < tiles_y - 1, col > 0
    has_later, has_earlier = window < windows - 1, window > 0
    to_east, to_west = {"space": place + tiles_y}, {"space": place - tiles_y}
    to_north, to_south = {"space": place + 1}, {"space": place - 1}
    to_later, to_earlier = {"tm": window + 1}, {"tm": window - 1}

    loads = [
        pltpu.make_async_copy(ref, raw.at[k], load_sem.at[k])
        for k, ref in enumerate((flow_x_hbm, flow_y_hbm, start_hbm))
    ]
    for load in loads:
        load.start()
    barrier = pltpu.get_barrier_semaphore()
    links = (
        (to_east, has_east),
        (to_west, has_west),
        (to_north, has_north),
        (to_south, has_south),
        (to_later, has_later),
        (to_earlier, has_earlier),
    )
    count = 0
    for device, there in links:
        @pl.when(there)
        def _():
            pl.semaphore_signal(barrier, inc=1, device_id=device, device_id_type=MESH)

        count = count + there.astype(jnp.int32)

    zero_row = jnp.zeros((SLABS, 128), f32)
    for ref in (fields.at[0], other):
        side_rows(ref, FIRST - 1)[...] = zero_row
        side_rows(ref, FIRST + ROWS_X)[...] = zero_row
    zero_x = jnp.zeros((STEPS * SLABS, 128), f32)
    zero_y = jnp.zeros((STEPS * 8, 128), f32)
    for k in range(ITERS):
        for side, there in ((0, has_east), (1, has_west)):
            @pl.when(jnp.logical_not(there))
            def _():
                x_in[k, side] = zero_x

        for side, there in ((0, has_south), (1, has_north)):
            @pl.when(jnp.logical_not(there))
            def _():
                y_in[k, side] = zero_y

    lane = lane_ids()
    sub = lax.broadcasted_iota(jnp.int32, (8, 128), 0)
    east_keep = jnp.where(sub == 7, has_east.astype(f32) * KEEP, 0.0)
    west_keep = jnp.where(sub == 0, has_west.astype(f32) * KEEP, 0.0)
    north_keep = jnp.where(lane >= 128 - SIDE, has_north.astype(f32) * KEEP, 0.0)
    south_keep = jnp.where(lane < SIDE, has_south.astype(f32) * KEEP, 0.0)

    def gathered(which, group, iz):
        rows = [(SIDE * zb + iz) * ROWS_X + 8 * group for zb in range(SIDE)]
        return swapped([raw[which, r : r + 8, :] for r in rows])

    loads[0].wait()
    loads[1].wait()
    mix = HORIZ / VERT
    for group in range(GROUPS):
        own = slice(8 * group, 8 * group + 8)
        for iz in range(SIDE):
            flow_x, flow_y = gathered(0, group, iz), gathered(1, group, iz)
            for iy in range(SIDE):
                slab = SIDE * iz + iy
                cx, cy = flow_x[iy] * (1.0 / VERT), flow_y[iy] * (1.0 / VERT)
                a = mix - jnp.minimum(cx, 0.0)
                b = mix + jnp.maximum(cx, 0.0)
                c = mix - jnp.minimum(cy, 0.0)
                d = mix + jnp.maximum(cy, 0.0)
                e = ((1.0 - 4.0 * HORIZ - 2.0 * VERT) / VERT - jnp.abs(cx)) - jnp.abs(cy)
                if group == GROUPS - 1:
                    e = e + a * east_keep
                if group == 0:
                    e = e + b * west_keep
                if iy == SIDE - 1:
                    e = e + c * north_keep
                if iy == 0:
                    e = e + d * south_keep
                a_ref[slab, own, :] = a
                b_ref[slab, own, :] = b
                c_ref[slab, own, :] = c
                d_ref[slab, own, :] = d
                e_ref[slab, own, :] = e
    loads[2].wait()
    for group in range(GROUPS):
        for iz in range(SIDE):
            start = gathered(2, group, iz)
            for iy in range(SIDE):
                base = (SIDE * iz + iy) * PADDED + FIRST + 8 * group
                fields[0, base : base + 8, :] = start[iy]

    @pl.when(jnp.logical_not(has_earlier))
    def _():
        for k in range(ITERS):
            for slab in range(SLABS):
                inside = slice(slab * PADDED + FIRST, slab * PADDED + FIRST + ROWS_X)
                fields[k + 1, inside, :] = fields[0, inside, :]

    coefs = (a_ref, b_ref, c_ref, d_ref, e_ref)

    def routed(source, target, sent, received, device, leaves, arrives):
        copy = pltpu.make_async_remote_copy(
            src_ref=source,
            dst_ref=target,
            send_sem=sent,
            recv_sem=received,
            device_id=device,
            device_id_type=MESH,
        )
        return copy, leaves, arrives

    def sides(k, part):
        x_part = pl.ds(part * SPAN * SLABS, SPAN * SLABS)
        y_part = pl.ds(part * SPAN * 8, SPAN * 8)
        routes = (
            (x_out.at[k, 0, x_part], x_in.at[k, 1, x_part], to_east, has_east, has_west),
            (x_out.at[k, 1, x_part], x_in.at[k, 0, x_part], to_west, has_west, has_east),
            (y_out.at[k, y_part], y_in.at[k, 1, y_part], to_south, has_south, has_north),
            (y_out.at[k, y_part], y_in.at[k, 0, y_part], to_north, has_north, has_south),
        )
        return [
            routed(source, target, send_sem.at[k, part, n], recv_sem.at[k, part, n], *rest)
            for n, (source, target, *rest) in enumerate(routes)
        ]

    def ended(k):
        inside = slice(FIRST, FIRST + ROWS_X)
        source, target = (
            fields.at[n].reshape(SLABS, PADDED, 128).at[:, inside, :] for n in (k, k + 1)
        )
        return [
            routed(
                source, target, field_sem.at[0, k], field_sem.at[1, k], to_later, has_later, has_earlier
            )
        ]

    def start(copies):
        for copy, leaves, _ in copies:
            pl.when(leaves)(copy.start)

    def arrive(copies):
        for copy, _, arrives in copies:
            pl.when(arrives)(copy.wait_recv)

    def leave(copies):
        for copy, leaves, _ in copies:
            pl.when(leaves)(copy.wait_send)

    for sweep in range(ITERS + 1):
        field = fields.at[sweep]
        ghosts = offers = None
        if sweep > 0:
            k = sweep - 1
            ghosts = (x_in.at[k, 0], x_in.at[k, 1], y_in.at[k, 0], y_in.at[k, 1])
            arrive(ended(k))
        if sweep < ITERS:
            offers = (x_out.at[sweep, 0], x_out.at[sweep, 1], y_out.at[sweep])

        def run(part, scale=None):
            if sweep > 0:
                arrive(sides(sweep - 1, part))
            for n in range(0, SPAN, 2):
                t = part * SPAN + n
                last = scale if n == SPAN - 2 else None
                step(field, other, t, coefs, ghosts, offers, None)
                step(other, field, t + 1, coefs, ghosts, offers, last)

        @pl.loop(0, SPANS - 1)
        def _(part):
            run(part)
            if sweep == 0:
                @pl.when(part == 0)
                def _():
                    pl.semaphore_wait(barrier, count)

            if sweep < ITERS:
                start(sides(sweep, part))

        run(SPANS - 1, RESCALE)
        if sweep < ITERS:
            start(sides(sweep, SPANS - 1))
            start(ended(sweep))

    for group in range(GROUPS):
        for iz in range(SIDE):
            base = [(SIDE * iz + iy) * PADDED + FIRST + 8 * group for iy in range(SIDE)]
            final = swapped([fields[ITERS, b : b + 8, :] for b in base])
            for zb in range(SIDE):
                r = (SIDE * zb + iz) * ROWS_X + 8 * group
                out[r : r + 8, :] = final[zb]
    for k in range(ITERS):
        leave(ended(k))

        @pl.loop(0, SPANS)
        def _(part):
            leave(sides(k, part))


def body(window_start, courant_x, courant_y):
    cells = (LEVELS * ROWS_X, ROWS_Y)
    coef = pltpu.VMEM((SLABS, ROWS_X, 128), f32)
    ended = pl.pallas_call(
        functools.partial(kernel, lax.axis_size("space") // TILES_X, lax.axis_size("tm")),
        out_shape=jax.ShapeDtypeStruct(cells, f32),
        in_specs=[pl.BlockSpec(memory_space=pltpu.HBM)] * 3,
        out_specs=pl.BlockSpec(memory_space=pltpu.VMEM),
        scratch_shapes=[
            pltpu.VMEM((3,) + cells, f32),
            pltpu.VMEM((ITERS + 1, SLABS * PADDED, 128), f32),
            pltpu.VMEM((SLABS * PADDED, 128), f32),
            coef,
            coef,
            coef,
            coef,
            coef,
            pltpu.VMEM((ITERS, 2, STEPS * SLABS, 128), f32),
            pltpu.VMEM((ITERS, 2, STEPS * SLABS, 128), f32),
            pltpu.VMEM((ITERS, STEPS * 8, 128), f32),
            pltpu.VMEM((ITERS, 2, STEPS * 8, 128), f32),
            pltpu.SemaphoreType.DMA((3,)),
            pltpu.SemaphoreType.DMA((ITERS, SPANS, 4)),
            pltpu.SemaphoreType.DMA((ITERS, SPANS, 4)),
            pltpu.SemaphoreType.DMA((2, ITERS)),
        ],
        compiler_params=pltpu.CompilerParams(
            collective_id=0, has_side_effects=True, vmem_limit_bytes=107 << 19
        ),
    )(window_start.reshape(cells), courant_x.reshape(cells), courant_y.reshape(cells))
    return ended.reshape(window_start.shape)


def solution(mesh):
    spec = P("tm", "space", None, None, None)
    return jax.shard_map(
        body, mesh=mesh, in_specs=(spec, spec, spec), out_specs=spec, check_vma=False
    )
```

```python
import functools

import jax
import jax.numpy as jnp
from jax import lax
from jax.experimental import pallas as pl
from jax.experimental.pallas import tpu as pltpu
from jax.sharding import PartitionSpec as P

STEPS = 16
ITERS = 2
TILES_X = 8
LEVELS, ROWS_X, ROWS_Y = 16, 32, 128
SIDE = 4
SLABS = SIDE * SIDE
FIRST = 8
PADDED = ROWS_X + 16
GROUPS = ROWS_X // 8
SPAN = 4
SPANS = STEPS // SPAN

HORIZ, VERT, ROBIN = 0.06, 0.08, 0.6
KEEP = (1.0 - 0.5 * ROBIN) / (1.0 + 0.5 * ROBIN)
INNER = (1.5 * ROBIN - 1.0) / (1.0 + 0.5 * ROBIN)
SECOND = (1.0 - 0.5 * ROBIN) / (1.0 + 0.5 * ROBIN)
RESCALE = VERT**STEPS

MESH = pl.DeviceIdType.MESH
f32 = jnp.float32


def lane_ids():
    return lax.broadcasted_iota(jnp.int32, (8, 128), 1)


def turn(x, by):
    return pltpu.roll(x, by % 128, 1) if by % 128 else x


def swapped(v):
    lane = lane_ids()
    low, high = lane % 2 == 0, lane % 4 < 2
    t0 = jnp.where(low, v[0], turn(v[1], 1))
    t1 = jnp.where(low, turn(v[0], -1), v[1])
    t2 = jnp.where(low, v[2], turn(v[3], 1))
    t3 = jnp.where(low, turn(v[2], -1), v[3])
    return (
        jnp.where(high, t0, turn(t2, 2)),
        jnp.where(high, t1, turn(t3, 2)),
        jnp.where(high, turn(t0, -2), t2),
        jnp.where(high, turn(t1, -2), t3),
    )


def side_rows(ref, row):
    return ref.at[pl.ds(row, SLABS, stride=PADDED), :]


def step(src, dst, t, coefs, ghosts, offers, scale):
    a_ref, b_ref, c_ref, d_ref, e_ref = coefs
    lane = lane_ids()
    north_side, south_side = lane >= 128 - SIDE, lane < SIDE
    top, bottom = lane % SIDE == SIDE - 1, lane % SIDE == 0
    south_data = lane % 8 < SIDE

    if offers is not None:
        east_out, west_out, y_out = offers
        west_out[pl.ds(t * SLABS, SLABS), :] = (
            side_rows(src, FIRST)[...] * INNER + side_rows(src, FIRST + 1)[...] * SECOND
        )
        east_out[pl.ds(t * SLABS, SLABS), :] = (
            side_rows(src, FIRST + ROWS_X - 1)[...] * INNER
            + side_rows(src, FIRST + ROWS_X - 2)[...] * SECOND
        )
    if ghosts is not None:
        east_in, west_in, south_in, north_in = ghosts
        side_rows(src, FIRST - 1)[...] = west_in[pl.ds(t * SLABS, SLABS), :]
        side_rows(src, FIRST + ROWS_X)[...] = east_in[pl.ds(t * SLABS, SLABS), :]
        both = jnp.where(
            south_data,
            turn(north_in[pl.ds(t * 8, 8), :], -SIDE),
            turn(south_in[pl.ds(t * 8, 8), :], SIDE),
        )

    packed = None
    for group in range(GROUPS):
        own = slice(8 * group, 8 * group + 8)
        f = []
        for iz in range(SIDE):
            base = [(SIDE * iz + iy) * PADDED + FIRST + 8 * group for iy in range(SIDE)]
            f.append([src[b : b + 8, :] for b in base])
        for iz in range(SIDE):
            spot = SIDE * group + iz
            ghost = 0.0 if ghosts is None else turn(both, -8 * spot - SIDE)
            past_north = jnp.where(north_side, ghost, turn(f[iz][0], -SIDE))
            past_south = jnp.where(south_side, ghost, turn(f[iz][3], SIDE))
            plus_y = f[iz][1:] + [past_north]
            minus_y = [past_south] + f[iz][:-1]
            for iy in range(SIDE):
                slab = SIDE * iz + iy
                base = slab * PADDED + FIRST + 8 * group
                if iz == SIDE - 1:
                    plus_z = jnp.where(top, f[iz][iy], turn(f[0][iy], -1))
                else:
                    plus_z = f[iz + 1][iy]
                if iz == 0:
                    minus_z = jnp.where(bottom, f[iz][iy], turn(f[SIDE - 1][iy], 1))
                else:
                    minus_z = f[iz - 1][iy]
                new = (
                    (
                        a_ref[slab, own, :] * src[base + 1 : base + 9, :]
                        + b_ref[slab, own, :] * src[base - 1 : base + 7, :]
                    )
                    + (c_ref[slab, own, :] * plus_y[iy] + d_ref[slab, own, :] * minus_y[iy])
                    + (e_ref[slab, own, :] * f[iz][iy] + (plus_z + minus_z))
                )
                if scale is not None:
                    new = new * scale
                dst[base : base + 8, :] = new
            if offers is not None:
                first = jnp.where(north_side, f[iz][3], f[iz][0])
                second = jnp.where(north_side, f[iz][2], f[iz][1])
                offer = turn(second + first * (INNER / SECOND), 8 * spot + SIDE)
                packed = offer if packed is None else jnp.where(lane // 8 == spot, offer, packed)
    if offers is not None:
        y_out[pl.ds(t * 8, 8), :] = packed * SECOND


def kernel(
    tiles_y,
    windows,
    start_hbm,
    flow_x_hbm,
    flow_y_hbm,
    out,
    raw,
    fields,
    other,
    a_ref,
    b_ref,
    c_ref,
    d_ref,
    e_ref,
    x_out,
    x_in,
    y_out,
    y_in,
    load_sem,
    send_sem,
    recv_sem,
    field_sem,
):
    window = lax.axis_index("tm")
    place = lax.axis_index("space")
    row, col = place // tiles_y, place % tiles_y
    has_east, has_west = row < TILES_X - 1, row > 0
    has_north, has_south = col < tiles_y - 1, col > 0
    has_later, has_earlier = window < windows - 1, window > 0
    to_east, to_west = {"space": place + tiles_y}, {"space": place - tiles_y}
    to_north, to_south = {"space": place + 1}, {"space": place - 1}
    to_later, to_earlier = {"tm": window + 1}, {"tm": window - 1}

    loads = [
        pltpu.make_async_copy(ref, raw.at[k], load_sem.at[k])
        for k, ref in enumerate((flow_x_hbm, flow_y_hbm, start_hbm))
    ]
    for load in loads:
        load.start()
    barrier = pltpu.get_barrier_semaphore()
    links = (
        (to_east, has_east),
        (to_west, has_west),
        (to_north, has_north),
        (to_south, has_south),
        (to_later, has_later),
        (to_earlier, has_earlier),
    )
    count = 0
    for device, there in links:
        @pl.when(there)
        def _():
            pl.semaphore_signal(barrier, inc=1, device_id=device, device_id_type=MESH)

        count = count + there.astype(jnp.int32)

    zero_row = jnp.zeros((SLABS, 128), f32)
    for ref in (fields.at[0], other):
        side_rows(ref, FIRST - 1)[...] = zero_row
        side_rows(ref, FIRST + ROWS_X)[...] = zero_row
    zero_x = jnp.zeros((STEPS * SLABS, 128), f32)
    zero_y = jnp.zeros((STEPS * 8, 128), f32)
    for k in range(ITERS):
        for side, there in ((0, has_east), (1, has_west)):
            @pl.when(jnp.logical_not(there))
            def _():
                x_in[k, side] = zero_x

        for side, there in ((0, has_south), (1, has_north)):
            @pl.when(jnp.logical_not(there))
            def _():
                y_in[k, side] = zero_y

    lane = lane_ids()
    sub = lax.broadcasted_iota(jnp.int32, (8, 128), 0)
    east_keep = jnp.where(sub == 7, has_east.astype(f32) * KEEP, 0.0)
    west_keep = jnp.where(sub == 0, has_west.astype(f32) * KEEP, 0.0)
    north_keep = jnp.where(lane >= 128 - SIDE, has_north.astype(f32) * KEEP, 0.0)
    south_keep = jnp.where(lane < SIDE, has_south.astype(f32) * KEEP, 0.0)

    def gathered(which, group, iz):
        rows = [(SIDE * zb + iz) * ROWS_X + 8 * group for zb in range(SIDE)]
        return swapped([raw[which, r : r + 8, :] for r in rows])

    loads[0].wait()
    loads[1].wait()
    mix = HORIZ / VERT
    for group in range(GROUPS):
        own = slice(8 * group, 8 * group + 8)
        for iz in range(SIDE):
            flow_x, flow_y = gathered(0, group, iz), gathered(1, group, iz)
            for iy in range(SIDE):
                slab = SIDE * iz + iy
                cx, cy = flow_x[iy] * (1.0 / VERT), flow_y[iy] * (1.0 / VERT)
                a = mix - jnp.minimum(cx, 0.0)
                b = mix + jnp.maximum(cx, 0.0)
                c = mix - jnp.minimum(cy, 0.0)
                d = mix + jnp.maximum(cy, 0.0)
                e = ((1.0 - 4.0 * HORIZ - 2.0 * VERT) / VERT - jnp.abs(cx)) - jnp.abs(cy)
                if group == GROUPS - 1:
                    e = e + a * east_keep
                if group == 0:
                    e = e + b * west_keep
                if iy == SIDE - 1:
                    e = e + c * north_keep
                if iy == 0:
                    e = e + d * south_keep
                a_ref[slab, own, :] = a
                b_ref[slab, own, :] = b
                c_ref[slab, own, :] = c
                d_ref[slab, own, :] = d
                e_ref[slab, own, :] = e
    loads[2].wait()
    for group in range(GROUPS):
        for iz in range(SIDE):
            start = gathered(2, group, iz)
            for iy in range(SIDE):
                base = (SIDE * iz + iy) * PADDED + FIRST + 8 * group
                fields[0, base : base + 8, :] = start[iy]

    @pl.when(jnp.logical_not(has_earlier))
    def _():
        for k in range(ITERS):
            for slab in range(SLABS):
                inside = slice(slab * PADDED + FIRST, slab * PADDED + FIRST + ROWS_X)
                fields[k + 1, inside, :] = fields[0, inside, :]

    coefs = (a_ref, b_ref, c_ref, d_ref, e_ref)

    def routed(source, target, sent, received, device, leaves, arrives):
        copy = pltpu.make_async_remote_copy(
            src_ref=source,
            dst_ref=target,
            send_sem=sent,
            recv_sem=received,
            device_id=device,
            device_id_type=MESH,
        )
        return copy, leaves, arrives

    def sides(k, part):
        x_part = pl.ds(part * SPAN * SLABS, SPAN * SLABS)
        y_part = pl.ds(part * SPAN * 8, SPAN * 8)
        routes = (
            (x_out.at[k, 0, x_part], x_in.at[k, 1, x_part], to_east, has_east, has_west),
            (x_out.at[k, 1, x_part], x_in.at[k, 0, x_part], to_west, has_west, has_east),
            (y_out.at[k, y_part], y_in.at[k, 1, y_part], to_south, has_south, has_north),
            (y_out.at[k, y_part], y_in.at[k, 0, y_part], to_north, has_north, has_south),
        )
        return [
            routed(source, target, send_sem.at[k, part, n], recv_sem.at[k, part, n], *rest)
            for n, (source, target, *rest) in enumerate(routes)
        ]

    def ended(k):
        inside = slice(FIRST, FIRST + ROWS_X)
        source, target = (
            fields.at[n].reshape(SLABS, PADDED, 128).at[:, inside, :] for n in (k, k + 1)
        )
        return [
            routed(
                source, target, field_sem.at[0, k], field_sem.at[1, k], to_later, has_later, has_earlier
            )
        ]

    def start(copies):
        for copy, leaves, _ in copies:
            pl.when(leaves)(copy.start)

    def arrive(copies):
        for copy, _, arrives in copies:
            pl.when(arrives)(copy.wait_recv)

    def leave(copies):
        for copy, leaves, _ in copies:
            pl.when(leaves)(copy.wait_send)

    for sweep in range(ITERS + 1):
        field = fields.at[sweep]
        ghosts = offers = None
        if sweep > 0:
            k = sweep - 1
            ghosts = (x_in.at[k, 0], x_in.at[k, 1], y_in.at[k, 0], y_in.at[k, 1])
            arrive(ended(k))
        if sweep < ITERS:
            offers = (x_out.at[sweep, 0], x_out.at[sweep, 1], y_out.at[sweep])

        def run(part, scale=None):
            if sweep > 0:
                arrive(sides(sweep - 1, part))
            for n in range(0, SPAN, 2):
                t = part * SPAN + n
                last = scale if n == SPAN - 2 else None
                step(field, other, t, coefs, ghosts, offers, None)
                step(other, field, t + 1, coefs, ghosts, offers, last)

        @pl.loop(0, SPANS - 1)
        def _(part):
            run(part)
            if sweep == 0:
                @pl.when(part == 0)
                def _():
                    pl.semaphore_wait(barrier, count)

            if sweep < ITERS:
                start(sides(sweep, part))

        run(SPANS - 1, RESCALE)
        if sweep < ITERS:
            last = [ended(sweep), sides(sweep, SPANS - 1)]
            for copies in last[::-1] if sweep == 0 else last:
                start(copies)

    for group in range(GROUPS):
        for iz in range(SIDE):
            base = [(SIDE * iz + iy) * PADDED + FIRST + 8 * group for iy in range(SIDE)]
            final = swapped([fields[ITERS, b : b + 8, :] for b in base])
            for zb in range(SIDE):
                r = (SIDE * zb + iz) * ROWS_X + 8 * group
                out[r : r + 8, :] = final[zb]
    for k in range(ITERS):
        leave(ended(k))

        @pl.loop(0, SPANS)
        def _(part):
            leave(sides(k, part))


def body(window_start, courant_x, courant_y):
    cells = (LEVELS * ROWS_X, ROWS_Y)
    coef = pltpu.VMEM((SLABS, ROWS_X, 128), f32)
    ended = pl.pallas_call(
        functools.partial(kernel, lax.axis_size("space") // TILES_X, lax.axis_size("tm")),
        out_shape=jax.ShapeDtypeStruct(cells, f32),
        in_specs=[pl.BlockSpec(memory_space=pltpu.HBM)] * 3,
        out_specs=pl.BlockSpec(memory_space=pltpu.VMEM),
        scratch_shapes=[
            pltpu.VMEM((3,) + cells, f32),
            pltpu.VMEM((ITERS + 1, SLABS * PADDED, 128), f32),
            pltpu.VMEM((SLABS * PADDED, 128), f32),
            coef,
            coef,
            coef,
            coef,
            coef,
            pltpu.VMEM((ITERS, 2, STEPS * SLABS, 128), f32),
            pltpu.VMEM((ITERS, 2, STEPS * SLABS, 128), f32),
            pltpu.VMEM((ITERS, STEPS * 8, 128), f32),
            pltpu.VMEM((ITERS, 2, STEPS * 8, 128), f32),
            pltpu.SemaphoreType.DMA((3,)),
            pltpu.SemaphoreType.DMA((ITERS, SPANS, 4)),
            pltpu.SemaphoreType.DMA((ITERS, SPANS, 4)),
            pltpu.SemaphoreType.DMA((2, ITERS)),
        ],
        compiler_params=pltpu.CompilerParams(
            collective_id=0, has_side_effects=True, vmem_limit_bytes=107 << 19
        ),
    )(window_start.reshape(cells), courant_x.reshape(cells), courant_y.reshape(cells))
    return ended.reshape(window_start.shape)


def solution(mesh):
    spec = P("tm", "space", None, None, None)
    return jax.shard_map(
        body, mesh=mesh, in_specs=(spec, spec, spec), out_specs=spec, check_vma=False
    )
```
